256 devices in a mesh: rep: 32 (over z, x_hi, core), col: 8 (over y, x_lo).
Axes of the slice: x: 4 (x_hi: 2, x_lo: 2; x = x_hi * 2 + x_lo), y: 4, z: 8, core: 2. Of those that a mesh axis runs over, the one named last changes fastest.
Arguments:
- x_rows: bfloat16 [65536, 1024], P(('rep', 'col')), may hold values from -6 to 6
- grad_out: bfloat16 [65536, 12288], P('rep', 'col'), may hold values from -0.125 to 0.125
- momentum: bfloat16 [32, 1024, 12288], P('rep', None, 'col'), may hold values from -6 to 6
- band: int32 [32], replicated, may hold values from 0 to 63, as said below
Outputs:
- new_momentum: bfloat16 [32, 1024, 12288], P('rep', None, 'col')
- update: bfloat16 [1024, 12288], P(None, 'col')
The draws below stay inside these ranges and needn't reach their ends.
Inputs may be any that keep to these rules, and one draw needn't show every extreme that they name: `band`: 32 distinct indices, all below 64; 0 and 63 are always among them.
All inputs are finite; a program needn't handle non-finite values.
Results may differ from the reference program's by a relative error of at most 0.001.
Values may be sent and summed in bfloat16 or wider, within the bound.
No kernel may reach another device: no remote copies, remote signals or barrier semaphores. Data moves between devices by JAX's collectives and lax.ppermute only.
A program may use at most 192 MiB of HBM per device.

```python
import math
import jax
import jax.numpy as jnp
from jax import lax

FF = 12288
ROWS = 1024
GROUP = 256
BAND = 32
TOK_DEV = 256
TOKENS = 65536
N_REP = 32
N_COL = 8


def draw_band(key, part):
    key = jax.random.fold_in(key, 11)
    others = jax.random.permutation(key, 62)[:BAND - 2].astype(jnp.int32) + 1
    return jnp.concatenate([jnp.zeros((1,), jnp.int32), others, jnp.full((1,), 63, jnp.int32)])


def level_of(stream_key, extent, shards, least, largest):
    def one(axis_at, blocks):
        draws = jax.random.uniform(jax.random.fold_in(jax.random.fold_in(stream_key, 6), axis_at), (blocks,), jnp.float32, least / len(shards), largest / len(shards))
        return jnp.repeat(jnp.exp(draws), extent[axis_at] // blocks).reshape((-1,) + (1,) * (len(extent) - axis_at - 1))

    gain = one(*shards[0])
    for cut in shards[1:]:
        gain = gain * one(*cut)
    return gain


def noise(key, dims, deviation, reach, pieces=(), kind=jnp.bfloat16):
    values = deviation * jax.random.normal(key, dims, jnp.float32)
    if pieces:
        values = values * level_of(key, dims, pieces, -0.22, 0.18)
    return jnp.clip(values, -reach, reach).astype(kind)


def setup_inputs(seed: int = 0) -> dict:
    key_list = jax.random.split(jax.random.key(seed), 5)
    x_rows = noise(key_list[0], (TOKENS, ROWS), 1.0, 6.0, ((0, 256),))
    grad_out = noise(key_list[1], (TOKENS, FF), (TOK_DEV * N_COL) ** -0.5, 0.125, ((0, 32), (1, 8)))
    momentum = noise(key_list[2], (N_REP, ROWS, FF), 1.0, 6.0, ((0, 32), (2, 8)))
    band = draw_band(jax.random.fold_in(key_list[4], 71), 0)
    return {"x_rows": x_rows, "grad_out": grad_out, "momentum": momentum, "band": band}


def dct_rows(band):
    index = band.astype(jnp.float32)[:, None]
    cells = jnp.arange(GROUP, dtype=jnp.float32)[None, :]
    factor = jnp.where(band == 0, math.sqrt(1.0 / GROUP), math.sqrt(2.0 / GROUP)).astype(jnp.float32)
    return factor[:, None] * jnp.cos(math.pi * (cells + 0.5) * index / GROUP)

def reference(x_rows, grad_out, momentum, band):
    basis = dct_rows(band)
    per_rep = TOK_DEV * N_COL
    inputs = x_rows.reshape(N_REP, per_rep, ROWS)
    cotangents = grad_out.reshape(N_REP, per_rep, FF)

    def one_replica(item):
        inputs_r, cotangents_r, momentum_r = item
        grad = jnp.dot(inputs_r.T, cotangents_r, preferred_element_type=jnp.float32)
        blended = 0.9 * momentum_r.astype(jnp.float32) + grad
        blocks = blended.reshape(ROWS, FF // GROUP, GROUP)
        coefficients = jnp.einsum('ibn,kn->ibk', blocks, basis, precision=lax.Precision.HIGHEST)
        decoded = jnp.einsum('ibk,kn->ibn', coefficients, basis, precision=lax.Precision.HIGHEST)
        fresh = (blended - decoded.reshape(ROWS, FF)).astype(jnp.bfloat16)
        return (fresh, coefficients)
    new_momentum, coefficients = lax.map(one_replica, (inputs, cotangents, momentum))
    summed = lax.optimization_barrier(jnp.sum(coefficients, axis=0))
    update = jnp.einsum('ibk,kn->ibn', summed, basis, precision=lax.Precision.HIGHEST)
    return (new_momentum, update.reshape(ROWS, FF).astype(jnp.bfloat16))
```

```python
import functools
import math

import jax
import jax.numpy as jnp
from jax import lax
from jax.experimental import pallas as pl
from jax.experimental.pallas import tpu as pltpu
from jax.sharding import Mesh
from jax.sharding import PartitionSpec as P

GROUP = 256
TILE = 512
F32 = jnp.float32
BF16 = jnp.bfloat16
PAIR = [(0, 1), (1, 0)]


def ring(size, step):
    return [(i, (i + step) % size) for i in range(size)]


def dct_rows(band, length):
    index = band.astype(F32)[:, None]
    cells = jnp.arange(length, dtype=F32)[None, :]
    factor = jnp.where(band == 0, math.sqrt(1.0 / length), math.sqrt(2.0 / length)).astype(F32)
    return factor[:, None] * jnp.cos(math.pi * (cells + 0.5) * index / length)


def split(value):
    high = value.astype(BF16)
    return high, (value - high.astype(F32)).astype(BF16)


def dot(a, b, dims):
    return lax.dot_general(a, b, ((dims[:1], dims[1:]), ((), ())), preferred_element_type=F32)


def decode(coefficients, stacked):
    high, low = split(coefficients)
    return dot(jnp.concatenate([high, low, high], axis=0), stacked, (0, 0))


def encode(pair, values, band):
    both = dot(pair, values, (1, 1))
    return both[:band] + both[band:]


def block(index, size):
    return slice(index * size, (index + 1) * size)


def load_kernel(band, grad_in, momentum, pair, coded, total, kept):
    blocks = total.shape[1] // GROUP
    for b in range(blocks):
        values = momentum[0, :, block(b, GROUP)]
        total[:, block(b, GROUP)] = 0.9 * values.astype(F32)
        kept[block(b, band), :] = 0.9 * encode(pair[...], values, band)
    for b in range(blocks):
        high, low = split(encode(pair[...], grad_in[:, block(b, GROUP)], band))
        coded[block(b, band), :] = high
        coded[block(blocks + b, band), :] = low


def tokens_of(place, count):
    return pl.ds(pl.multiple_of(place * count, count), count)


def chunks(groups, refs):
    taken, out = 0, []
    for count in groups:
        out.append(refs[taken : taken + count])
        taken += count
    return out, refs[taken:]


def take(pieces, columns):
    parts = [piece[:, columns] for piece in pieces]
    return parts[0] if len(parts) == 1 else jnp.concatenate(parts, axis=0)


def code_sum(places, xs, coded, columns):
    value = 0.0
    half = coded.shape[0] // 2
    for s, pieces in enumerate(xs):
        x = take(pieces, columns)
        tokens = tokens_of(places[s], x.shape[0])
        value = value + (dot(coded[:half, tokens], x, (1, 0)) + dot(coded[half:, tokens], x, (1, 0)))
    return value


def grad_sum(places, xs, grad_in, rows, columns):
    value = 0.0
    for s, pieces in enumerate(xs):
        x = take(pieces, rows)
        value = value + dot(x, grad_in[tokens_of(places[s], x.shape[0]), columns], (0, 0))
    return value


def add_kernel(groups, places, *refs):
    xs, refs = chunks(groups, refs)
    grad_in, coded, total, kept, total_out, kept_out = refs

    @pl.loop(0, total.shape[0] // TILE)
    def _(i):
        rows = pl.ds(pl.multiple_of(i * TILE, TILE), TILE)
        kept_out[:, rows] = kept[:, rows] + code_sum(places, xs, coded, rows)
        for b in range(total.shape[1] // TILE):
            columns = block(b, TILE)
            total_out[rows, columns] = total[rows, columns] + grad_sum(places, xs, grad_in, rows, columns)


def code_kernel(groups, places, core, *refs):
    xs, refs = chunks(groups, refs)
    coded, kept, kept_out, mine, other = refs
    rows = kept.shape[1] // 2

    def half(index, out):
        columns = pl.ds(pl.multiple_of(index * rows, rows), rows)
        value = kept[:, columns] + code_sum(places, xs, coded, columns)
        kept_out[:, columns] = value
        for t in range(rows // 128):
            out[block(t, value.shape[0]), :] = value[:, block(t, 128)]

    half(1 - core[0], other)
    half(core[0], mine)


def fresh_kernel(groups, band, places, *refs):
    xs, refs = chunks(groups, refs)
    grad_in, total, kept, stacked, fresh, staged, sems = refs
    steps = total.shape[0] // TILE
    for i in range(steps):
        rows = block(i, TILE)
        for b in range(total.shape[1] // GROUP):
            columns = block(b, GROUP)
            value = total[rows, columns] + grad_sum(places, xs, grad_in, rows, columns)
            value = value - decode(kept[block(b, band), rows], stacked[...])
            staged[rows, columns] = value.astype(BF16)
        pltpu.make_async_copy(staged.at[rows], fresh.at[0, rows], sems.at[i]).start()
    for i in range(steps):
        rows = block(i, TILE)
        pltpu.make_async_copy(staged.at[rows], fresh.at[0, rows], sems.at[i]).wait()


def part_kernel(chips, parts, spread):
    rows = parts.shape[0] // chips
    value = parts[:rows, :]
    for i in range(1, chips):
        value = value + parts[block(i, rows), :]
    for i in range(chips):
        spread[block(i, rows), :] = value


def update_kernel(band, core, mine, other, stacked, update):
    step = pl.program_id(0)
    kept = mine.shape[0] // 4
    value = jnp.where(step == core[0], mine[...], other[...])
    for b in range(update.shape[1] // GROUP):
        parts = [value[t * kept + b * band : t * kept + (b + 1) * band] for t in range(4)]
        update[:, block(b, GROUP)] = decode(jnp.concatenate(parts, axis=1), stacked[...]).astype(BF16)


VMEM = pl.BlockSpec(memory_space=pltpu.VMEM)
SMEM = pl.BlockSpec(memory_space=pltpu.SMEM)
ANY = pl.BlockSpec(memory_space=pl.ANY)


def params(mib):
    return pltpu.CompilerParams(vmem_limit_bytes=mib << 20)


def held(value):
    return pltpu.with_memory_space_constraint(value, pltpu.VMEM)


def estimate(flops, size):
    return pl.CostEstimate(flops=flops, bytes_accessed=size, transcendentals=0)


def load(grad_out, momentum, pair, band):
    tokens, columns = grad_out.shape
    rows = momentum.shape[1]
    kept = columns // GROUP * band
    return pl.pallas_call(
        functools.partial(load_kernel, band),
        in_specs=[VMEM] * 3,
        out_specs=[VMEM] * 3,
        out_shape=[
            pltpu.VMEM((2 * kept, tokens), BF16),
            pltpu.VMEM((rows, columns), F32),
            pltpu.VMEM((kept, rows), F32),
        ],
        compiler_params=params(16),
        cost_estimate=estimate(2 * columns * (tokens + rows) * 256, 0),
        name="load",
    )(held(grad_out), held(momentum), pair)


def flat(chunks):
    pieces = [piece for chunk in chunks for piece in chunk]
    return tuple(map(len, chunks)), pieces, len(pieces), sum(piece.shape[0] for piece in pieces)


def add(places, xs, grad_in, coded, total, kept):
    groups, xs, count, tokens = flat(xs)
    rows, columns = total.shape
    return pl.pallas_call(
        functools.partial(add_kernel, groups),
        in_specs=[SMEM] + [VMEM] * (count + 4),
        out_specs=[VMEM] * 2,
        out_shape=[pltpu.VMEM(total.shape, F32), pltpu.VMEM(kept.shape, F32)],
        input_output_aliases={count + 3: 0, count + 4: 1},
        compiler_params=params(16),
        cost_estimate=estimate(2 * tokens * rows * columns * 5 // 4, 0),
        name="add",
    )(places, *[held(x) for x in xs], held(grad_in), held(coded), held(total), held(kept))


def code(places, core, xs, coded, kept):
    groups, xs, count, tokens = flat(xs)
    size, rows = kept.shape
    out = jax.ShapeDtypeStruct((size * rows // 256, 128), F32)
    return pl.pallas_call(
        functools.partial(code_kernel, groups),
        in_specs=[SMEM, SMEM] + [VMEM] * (count + 2),
        out_specs=[VMEM] * 3,
        out_shape=[pltpu.VMEM(kept.shape, F32), pltpu.VMEM(out.shape, F32), pltpu.VMEM(out.shape, F32)],
        compiler_params=params(16),
        cost_estimate=estimate(2 * tokens * rows * size * 2, 0),
        name="code",
    )(places, core, *[held(x) for x in xs], held(coded), held(kept))


def finish(places, xs, grad_in, total, kept, stacked, band):
    groups, xs, count, tokens = flat(xs)
    rows, columns = total.shape
    return pl.pallas_call(
        functools.partial(fresh_kernel, groups, band),
        in_specs=[SMEM] + [VMEM] * (count + 4),
        out_specs=ANY,
        out_shape=jax.ShapeDtypeStruct((1, rows, columns), BF16),
        scratch_shapes=[pltpu.VMEM((rows, columns), BF16), pltpu.SemaphoreType.DMA((rows // TILE,))],
        compiler_params=params(16),
        cost_estimate=estimate(4 * tokens * rows * columns, rows * columns * 2),
        name="finish",
    )(places, *[held(x) for x in xs], held(grad_in), held(total), held(kept), stacked)


def sum_parts(parts, chips):
    return pl.pallas_call(
        functools.partial(part_kernel, chips),
        in_specs=[VMEM],
        out_specs=VMEM,
        out_shape=jax.ShapeDtypeStruct(parts.shape, F32),
        compiler_params=params(16),
        name="sum_parts",
    )(parts)


def make_update(core, mine, other, stacked, band, rows, columns):
    return pl.pallas_call(
        functools.partial(update_kernel, band),
        grid=(2,),
        in_specs=[SMEM]
        + [pl.BlockSpec(mine.shape, lambda i: (0, 0))] * 2
        + [pl.BlockSpec(stacked.shape, lambda i: (0, 0))],
        out_specs=pl.BlockSpec((rows // 2, columns), lambda i: (i, 0)),
        out_shape=jax.ShapeDtypeStruct((rows, columns), BF16),
        compiler_params=params(32),
        name="update",
    )(core, mine, other, stacked)


def shards(x_rows, grad_out, momentum, band_index):
    band = band_index.shape[0]
    basis = dct_rows(band_index, GROUP)
    rounded = lax.reduce_precision(basis, 8, 7)
    high, low = rounded.astype(BF16), (basis - rounded).astype(BF16)
    pair = jnp.concatenate([high, low], axis=0)
    stacked = jnp.concatenate([high, high, low], axis=0)

    y, xl = lax.axis_index("y"), lax.axis_index("xl")
    core = lax.axis_index("core").astype(jnp.int32).reshape(1)

    def places(*steps):
        return jnp.stack([((y + dy) % 4) * 2 + (xl + dx) % 2 for dy, dx in steps]).astype(jnp.int32)

    def across(v):
        return lax.ppermute(v, "xl", PAIR)

    def from_above(v):
        return lax.ppermute(v, "y", ring(4, -1))

    def from_below(v):
        return lax.ppermute(v, "y", ring(4, 1))

    near = places((0, 0), (0, 1), (1, 0), (3, 0))
    middle = places((1, 1), (3, 1), (2, 0))
    last = places((2, 1))
    pair, stacked, near, middle, last, core = lax.optimization_barrier((pair, stacked, near, middle, last, core))
    with jax.named_scope("gather_near"):
        xn, yp, ym = across(x_rows), from_above(x_rows), from_below(x_rows)
        sums = load(grad_out, momentum, pair, band)
        (xn, yp, ym), (coded, total, kept) = lax.optimization_barrier(((xn, yp, ym), sums))
    with jax.named_scope("gather_middle"):
        xyp, xym, y2 = lax.optimization_barrier((across(yp), from_below(xn), from_above(yp)))
    total, kept = add(near, [[x_rows], [xn], [yp], [ym]], grad_out, coded, total, kept)
    with jax.named_scope("gather_far"):
        cuts = (96, 176)
        xy2 = [across(y2[: cuts[0]]), from_above(xyp[cuts[0] : cuts[1]]), from_below(xym[cuts[1] :])]
    total, kept = add(middle, [[xyp], [xym], [y2]], grad_out, coded, total, kept)
    kept, mine, other = code(last, core, [xy2], coded, kept)
    with jax.named_scope("sum_core"):
        mine = mine + lax.ppermute(other, "core", PAIR)
    fresh = finish(last, [xy2], grad_out, total, kept, stacked, band)
    with jax.named_scope("sum_chips"):
        parts = lax.all_to_all(mine, ("z", "xh"), 0, 0, tiled=True)
    with jax.named_scope("spread_chips"):
        whole = lax.all_to_all(sum_parts(parts, 16), ("z", "xh"), 0, 0, tiled=True)
    with jax.named_scope("spread_core"):
        other = lax.ppermute(whole, "core", PAIR)
    return fresh, make_update(core, whole, other, stacked, band, *total.shape)


def solution(mesh):
    fine = Mesh(mesh.devices.reshape(8, 2, 2, 4, 2), ("z", "xh", "core", "y", "xl"))
    rep, col = ("z", "xh", "core"), ("y", "xl")
    return jax.shard_map(
        shards,
        mesh=fine,
        in_specs=(P(rep + col, None), P(rep, col), P(rep, None, col), P()),
        out_specs=(P(rep, None, col), P(None, col)),
        check_vma=False,
    )
```

```python
import functools
import math

import jax
import jax.numpy as jnp
from jax import lax
from jax.experimental import pallas as pl
from jax.experimental.pallas import tpu as pltpu
from jax.sharding import Mesh
from jax.sharding import PartitionSpec as P

GROUP = 256
TILE = 512
PAD = 16
F32 = jnp.float32
BF16 = jnp.bfloat16
PAIR = [(0, 1), (1, 0)]


def ring(size, step):
    return [(i, (i + step) % size) for i in range(size)]


def dct_rows(band, length):
    index = band.astype(F32)[:, None]
    cells = jnp.arange(length, dtype=F32)[None, :]
    factor = jnp.where(band == 0, math.sqrt(1.0 / length), math.sqrt(2.0 / length)).astype(F32)
    return factor[:, None] * jnp.cos(math.pi * (cells + 0.5) * index / length)


def split(value):
    high = value.astype(BF16)
    return high, (value - high.astype(F32)).astype(BF16)


def dot(a, b, dims):
    return lax.dot_general(a, b, ((dims[:1], dims[1:]), ((), ())), preferred_element_type=F32)


def decode(coefficients, stacked):
    high, low = split(coefficients)
    return dot(jnp.concatenate([high, low, high], axis=0), stacked, (0, 0))


def encode(pair, values, band):
    both = dot(pair, values, (1, 1))
    return both[:band] + both[band:]


def block(index, size):
    return slice(index * size, (index + 1) * size)


def load_kernel(band, place, grad_out, momentum, pair, x_rows, coded, kept, own, grad_in, total, momentum_in, sems):
    blocks = grad_in.shape[1] // GROUP
    halves = [block(h, grad_in.shape[0] // 2) for h in range(2)]
    ends = [(momentum.at[0], momentum_in)] + [(grad_out.at[h], grad_in.at[h]) for h in halves] + [(x_rows, own)]
    copies = [pltpu.make_async_copy(*pair, sems.at[c]) for c, pair in enumerate(ends)]
    for copy in copies:
        copy.start()
    copies[0].wait()
    for b in range(blocks):
        kept[block(b, band), :] = 0.9 * encode(pair[...], momentum_in[:, block(b, GROUP)], band)
    for copy, half in zip(copies[1:3], halves):
        copy.wait()
        for b in range(blocks):
            high, low = split(encode(pair[...], grad_in[half, block(b, GROUP)], band))
            coded[block(b, band), half] = high
            coded[block(blocks + b, band), half] = low
    copies[3].wait()
    for i in range(total.shape[0] // TILE):
        rows = block(i, TILE)
        kept[:, rows] = kept[:, rows] + code_sum(place, [[own]], coded, rows)
        for w in range(total.shape[1] // TILE):
            wide = block(w, TILE)
            start = 0.9 * momentum_in[rows, wide].astype(F32)
            total[rows, wide] = start + grad_sum(place, [[own]], grad_in, rows, wide)


def tokens_of(place, count):
    return pl.ds(pl.multiple_of(place * count, count), count)


def chunks(groups, refs):
    taken, out = 0, []
    for count in groups:
        out.append(refs[taken : taken + count])
        taken += count
    return out, refs[taken:]


def take(pieces, columns):
    parts = [piece[:, columns] for piece in pieces]
    return parts[0] if len(parts) == 1 else jnp.concatenate(parts, axis=0)


def code_sum(places, xs, coded, columns):
    value = 0.0
    half = coded.shape[0] // 2
    for s, pieces in enumerate(xs):
        x = take(pieces, columns)
        tokens = tokens_of(places[s], x.shape[0])
        value = value + (dot(coded[:half, tokens], x, (1, 0)) + dot(coded[half:, tokens], x, (1, 0)))
    return value


def grad_sum(places, xs, grad_in, rows, columns):
    value = 0.0
    for s, pieces in enumerate(xs):
        x = take(pieces, rows)
        value = value + dot(x, grad_in[tokens_of(places[s], x.shape[0]), columns], (0, 0))
    return value


def add_kernel(groups, span, places, *refs):
    xs, refs = chunks(groups, refs)
    grad_in, base = refs[:2]
    total, staged, sems = refs[-3:]
    copies = []
    for w in range(total.shape[1] // TILE):
        wide = block(w, TILE)
        staged[:, wide] = base[span, wide] + grad_sum(places, xs, grad_in, span, wide)
        copies.append(pltpu.make_async_copy(staged.at[:, wide], total.at[span, wide], sems.at[w]))
        copies[-1].start()
    for copy in copies:
        copy.wait()


def tally_kernel(groups, places, *refs):
    xs, refs = chunks(groups, refs)
    coded, kept, kept_out = refs
    half = kept.shape[1] // 2
    for i in range(2):
        rows = block(i, half)
        kept_out[:, rows] = kept[:, rows] + code_sum(places, xs, coded, rows)


def code_kernel(groups, places, core, *refs):
    xs, refs = chunks(groups, refs)
    coded, kept, kept_out, mine, other = refs
    rows = kept.shape[1] // 2

    def half(index, out):
        columns = pl.ds(pl.multiple_of(index * rows, rows), rows)
        value = kept[:, columns] + code_sum(places, xs, coded, columns)
        kept_out[:, columns] = value
        for t in range(rows // 128):
            out[block(t, value.shape[0]), :] = value[:, block(t, 128)]

    half(1 - core[0], other)
    half(core[0], mine)


def fresh_kernel(groups, band, places, *refs):
    count = sum(groups)
    xs, refs = refs[:count], refs[count:]
    grad_out, total, kept, stacked, fresh, x_in, g_in, total_in, kept_in, staged, sems, out_sems = refs
    rows, columns = total.shape
    steps, wides = rows // TILE, columns // TILE
    tokens = x_in.shape[0] // len(groups)
    ends = []
    ready = [[0] * wides for _ in range(steps)]
    for i in range(steps):
        span, start = block(i, TILE), 0
        for x in xs:
            ends.append((x.at[:, span], x_in.at[start : start + x.shape[0], span]))
            start += x.shape[0]
        for w in range(wides):
            wide = block(w, TILE)
            for s in range(len(groups) if i == 0 else 0):
                ends.append((grad_out.at[tokens_of(places[s], tokens), wide], g_in.at[block(s, tokens), wide]))
            ends.append((total.at[span, wide], total_in.at[span, wide]))
            if w == 0:
                ends.append((kept.at[:, span], kept_in.at[:, span]))
            ready[i][w] = len(ends)
    copies = [pltpu.make_async_copy(*pair, sems.at[i]) for i, pair in enumerate(ends)]
    for copy in copies:
        copy.start()
    waited, outs = 0, []
    for i in range(steps):
        span = block(i, TILE)
        for w in range(wides):
            for copy in copies[waited : ready[i][w]]:
                copy.wait()
            waited = ready[i][w]
            for b in range(w * TILE // GROUP, (w + 1) * TILE // GROUP):
                cols = block(b, GROUP)
                value = total_in[span, cols] + dot(x_in[:, span], g_in[:, cols], (0, 0))
                value = value - decode(kept_in[block(b, band), span], stacked[...])
                staged[span, cols] = value.astype(BF16)
        outs.append(pltpu.make_async_copy(staged.at[span], fresh.at[0, span], out_sems.at[i]))
        outs[-1].start()
    for out in outs:
        out.wait()


def join_kernel(mine, other, kept, out, kept_out, staged, sems):
    save = pltpu.make_async_copy(kept, kept_out, sems.at[0])
    staged[...] = mine[...] + other[...]
    give = pltpu.make_async_copy(staged, out, sems.at[1])
    give.start()
    save.start()
    give.wait()
    save.wait()


def part_kernel(chips, parts, spread):
    rows = parts.shape[0] // chips
    value = parts[:rows, :]
    for i in range(1, chips):
        value = value + parts[block(i, rows), :]
    largest = jnp.maximum(jnp.max(jnp.abs(value), axis=0, keepdims=True), 2.0**-100)
    power = jnp.ceil(jnp.log2(largest))
    level = jnp.round(value * jnp.exp2(15.0 - power))
    level = jnp.clip(level, -32767.0, 32767.0).astype(jnp.int32).astype(jnp.int16)
    power = jnp.broadcast_to(power, (PAD, value.shape[1])).astype(jnp.int32).astype(jnp.int16)
    for i in range(chips):
        start = i * (rows + PAD)
        spread[start : start + rows, :] = level
        spread[start + rows : start + rows + PAD, :] = power


def update_kernel(band, chips, where, whole, stacked, *refs):
    update = refs[-1]
    rows = whole.shape[0] // chips - PAD
    values = []
    for i in range(chips):
        start = i * (rows + PAD)
        level = whole[start : start + rows, :].astype(jnp.int32).astype(F32)
        power = whole[start + rows : start + rows + PAD, :].astype(jnp.int32).astype(F32)[:1]
        values.append(level * jnp.exp2(power - 15.0))
    value = jnp.concatenate(values, axis=0)
    tiles = update.shape[0] // 128
    kept = value.shape[0] // tiles
    for b in range(update.shape[1] // GROUP):
        parts = [value[t * kept + b * band : t * kept + (b + 1) * band] for t in range(tiles)]
        update[:, block(b, GROUP)] = decode(jnp.concatenate(parts, axis=1), stacked[...]).astype(BF16)


VMEM = pl.BlockSpec(memory_space=pltpu.VMEM)
SMEM = pl.BlockSpec(memory_space=pltpu.SMEM)
ANY = pl.BlockSpec(memory_space=pl.ANY)
HBM = pl.BlockSpec(memory_space=pltpu.HBM)


def params(mib):
    return pltpu.CompilerParams(vmem_limit_bytes=mib << 20)


def held(value):
    return pltpu.with_memory_space_constraint(value, pltpu.VMEM)


def far(value):
    return pltpu.with_memory_space_constraint(value, pltpu.HBM)


def estimate(flops, size):
    return pl.CostEstimate(flops=flops, bytes_accessed=size, transcendentals=0)


def load(place, grad_out, momentum, pair, x_rows, band):
    tokens, columns = grad_out.shape
    rows = momentum.shape[1]
    kept = columns // GROUP * band
    return pl.pallas_call(
        functools.partial(load_kernel, band),
        in_specs=[SMEM, ANY, ANY, VMEM, ANY],
        out_specs=[VMEM] * 5,
        out_shape=[
            pltpu.VMEM((2 * kept, tokens), BF16),
            pltpu.VMEM((kept, rows), F32),
            pltpu.VMEM(x_rows.shape, BF16),
            pltpu.VMEM(grad_out.shape, BF16),
            pltpu.VMEM((rows, columns), F32),
        ],
        scratch_shapes=[pltpu.VMEM((rows, columns), BF16), pltpu.SemaphoreType.DMA((4,))],
        compiler_params=params(16),
        cost_estimate=estimate(2 * columns * (tokens + rows) * 256, 2 * columns * (tokens + rows)),
        name="load",
    )(place, far(grad_out), far(momentum), pair, far(x_rows))


def flat(chunks):
    pieces = [piece for chunk in chunks for piece in chunk]
    return tuple(map(len, chunks)), pieces, len(pieces), sum(piece.shape[0] for piece in pieces)


def add(span, places, xs, grad_in, base, total=None):
    groups, xs, count, tokens = flat(xs)
    shape = base.shape
    rows = span.stop - span.start
    others = [] if total is None else [far(total)]
    return pl.pallas_call(
        functools.partial(add_kernel, groups, span),
        in_specs=[SMEM] + [VMEM] * (count + 2) + [ANY] * len(others),
        out_specs=ANY,
        out_shape=pltpu.HBM(shape, F32),
        input_output_aliases={count + 3: 0} if others else {},
        scratch_shapes=[pltpu.VMEM((rows, shape[1]), F32), pltpu.SemaphoreType.DMA((shape[1] // TILE,))],
        compiler_params=params(16),
        cost_estimate=estimate(2 * tokens * rows * shape[1], rows * shape[1] * 4),
        name="add",
    )(places, *[held(x) for x in xs], held(grad_in), held(base), *others)


def tally(places, xs, coded, kept):
    groups, xs, count, tokens = flat(xs)
    size, rows = kept.shape
    return pl.pallas_call(
        functools.partial(tally_kernel, groups),
        in_specs=[SMEM] + [VMEM] * (count + 2),
        out_specs=VMEM,
        out_shape=pltpu.VMEM(kept.shape, F32),
        compiler_params=params(16),
        cost_estimate=estimate(2 * tokens * rows * size * 2, 0),
        name="tally",
    )(places, *[held(x) for x in xs], held(coded), held(kept))


def code(places, core, xs, coded, kept):
    groups, xs, count, tokens = flat(xs)
    size, rows = kept.shape
    out = jax.ShapeDtypeStruct((size * rows // 256, 128), F32)
    return pl.pallas_call(
        functools.partial(code_kernel, groups),
        in_specs=[SMEM, SMEM] + [VMEM] * (count + 2),
        out_specs=[VMEM] * 3,
        out_shape=[pltpu.VMEM(kept.shape, F32), pltpu.VMEM(out.shape, F32), pltpu.VMEM(out.shape, F32)],
        compiler_params=params(16),
        cost_estimate=estimate(2 * tokens * rows * size * 2, 0),
        name="code",
    )(places, core, *[held(x) for x in xs], held(coded), held(kept))


def finish(places, xs, grad_out, total, kept, stacked, band):
    groups, xs, count, tokens = flat(xs)
    rows, columns = total.shape
    steps, wides = rows // TILE, columns // TILE
    loads = (count + 1) * steps + wides * (len(groups) + steps)
    return pl.pallas_call(
        functools.partial(fresh_kernel, groups, band),
        in_specs=[SMEM] + [ANY] * (count + 3) + [VMEM],
        out_specs=ANY,
        out_shape=jax.ShapeDtypeStruct((1, rows, columns), BF16),
        scratch_shapes=[
            pltpu.VMEM((tokens, rows), BF16),
            pltpu.VMEM((tokens, columns), BF16),
            pltpu.VMEM(total.shape, F32),
            pltpu.VMEM(kept.shape, F32),
            pltpu.VMEM((rows, columns), BF16),
            pltpu.SemaphoreType.DMA((loads,)),
            pltpu.SemaphoreType.DMA((steps,)),
        ],
        compiler_params=params(24),
        cost_estimate=estimate(4 * tokens * rows * columns, rows * columns * 6),
        name="finish",
    )(places, *map(far, xs), far(grad_out), far(total), far(kept), stacked)


def join(mine, other, kept):
    return pl.pallas_call(
        join_kernel,
        in_specs=[VMEM] * 3,
        out_specs=[ANY] * 2,
        out_shape=[pltpu.HBM(mine.shape, F32), pltpu.HBM(kept.shape, F32)],
        scratch_shapes=[pltpu.VMEM(mine.shape, F32), pltpu.SemaphoreType.DMA((2,))],
        compiler_params=params(4),
        name="join",
    )(held(mine), held(other), held(kept))


def sum_parts(parts, chips):
    return pl.pallas_call(
        functools.partial(part_kernel, chips),
        in_specs=[VMEM],
        out_specs=VMEM,
        out_shape=pltpu.VMEM((parts.shape[0] + chips * PAD, parts.shape[1]), jnp.int16),
        compiler_params=params(16),
        name="sum_parts",
    )(held(parts))


def make_update(where, whole, stacked, band, rows, columns, update=None):
    others = [] if update is None else [update]
    return pl.pallas_call(
        functools.partial(update_kernel, band, 8),
        grid_spec=pltpu.PrefetchScalarGridSpec(
            num_scalar_prefetch=1,
            grid=(2,),
            in_specs=[
                pl.BlockSpec((whole.shape[0] // 2, whole.shape[1]), lambda i, where: (i, 0)),
                pl.BlockSpec(stacked.shape, lambda i, where: (0, 0)),
            ]
            + [ANY] * len(others),
            out_specs=pl.BlockSpec((rows // 4, columns), lambda i, where: (2 * where[0] + i, 0)),
        ),
        out_shape=jax.ShapeDtypeStruct((rows, columns), BF16),
        input_output_aliases={3: 0} if others else {},
        compiler_params=params(16),
        cost_estimate=estimate(rows * columns * 96, rows * columns),
        name="update",
    )(where, whole, stacked, *others)


def shards(x_rows, grad_out, momentum, band_index):
    band = band_index.shape[0]
    basis = dct_rows(band_index, GROUP)
    rounded = lax.reduce_precision(basis, 8, 7)
    high, low = rounded.astype(BF16), (basis - rounded).astype(BF16)
    pair = jnp.concatenate([high, low], axis=0)
    stacked = jnp.concatenate([high, high, low], axis=0)

    y, xl = lax.axis_index("y"), lax.axis_index("xl")
    core = lax.axis_index("core").astype(jnp.int32).reshape(1)

    def places(*steps):
        return jnp.stack([((y + dy) % 4) * 2 + (xl + dx) % 2 for dy, dx in steps]).astype(jnp.int32)

    def across(v):
        return lax.ppermute(v, "xl", PAIR)

    def from_above(v):
        return lax.ppermute(v, "y", ring(4, -1))

    def from_below(v):
        return lax.ppermute(v, "y", ring(4, 1))

    first = places((0, 0))
    near = places((0, 1), (1, 0), (3, 0))
    middle = places((1, 1), (3, 1), (2, 0))
    last = places((2, 1))
    ends = places((1, 1), (3, 1), (2, 0), (2, 1))
    apart = 1 - core
    pair, stacked, first, near, middle, last, ends, core, apart = lax.optimization_barrier(
        (pair, stacked, first, near, middle, last, ends, core, apart)
    )
    with jax.named_scope("gather_near"):
        yp, xn, ym = from_above(x_rows), across(x_rows), from_below(x_rows)
        loaded = load(first, grad_out, momentum, pair, x_rows, band)
        yp, (coded, kept, own, grad_in, base) = lax.optimization_barrier((yp, loaded))
        xn, ym = lax.optimization_barrier((xn, ym))
    half = yp.shape[0] // 2
    with jax.named_scope("gather_middle"):
        y2 = [from_above(yp[:half])]
        xyp = across(yp)
        y2.append(from_above(yp[half:]))
        xym = [from_below(xn[half:])]
        xym.insert(0, from_below(xn[:half]))
    rows = momentum.shape[1]
    close = [[xn], [yp], [ym]]
    total = add(slice(0, rows // 2), near, close, grad_in, base)
    y2[0], xym[1], total = lax.optimization_barrier((y2[0], xym[1], total))
    with jax.named_scope("gather_far"):
        xy2 = [across(y2[0]), from_below(xym[1])]
    total = add(slice(rows // 2, rows), near, close, grad_in, base, total)
    kept = tally(near, close, coded, kept)
    kept = tally(middle, [[xyp], xym, y2], coded, kept)
    kept, total = lax.optimization_barrier((kept, total))
    kept, mine, other = code(last, core, [xy2], coded, kept)
    with jax.named_scope("sum_core"):
        mine, kept = join(mine, lax.ppermute(other, "core", PAIR), kept)
    with jax.named_scope("sum_chips"):
        parts = lax.all_to_all(mine, ("z", "xh"), 0, 0, tiled=True)
    fresh = finish(ends, [[xyp], xym, y2, xy2], grad_out, total, kept, stacked, band)
    parts, fresh = lax.optimization_barrier((parts, fresh))
    with jax.named_scope("spread_chips"):
        whole = lax.all_to_all(sum_parts(parts, 16), ("z", "xh"), 0, 0, tiled=True)
    with jax.named_scope("spread_core"):
        other = lax.ppermute(whole, "core", PAIR)
    update = make_update(core, whole, stacked, band, rows, grad_out.shape[1])
    return fresh, make_update(apart, other, stacked, band, rows, grad_out.shape[1], update)


def solution(mesh):
    fine = Mesh(mesh.devices.reshape(8, 2, 2, 4, 2), ("z", "xh", "core", "y", "xl"))
    rep, col = ("z", "xh", "core"), ("y", "xl")
    return jax.shard_map(
        shards,
        mesh=fine,
        in_specs=(P(rep + col, None), P(rep, col), P(rep, None, col), P()),
        out_specs=(P(rep, None, col), P(None, col)),
        check_vma=False,
    )
```

```python
import functools
import math

import jax
import jax.numpy as jnp
from jax import lax
from jax.experimental import pallas as pl
from jax.experimental.pallas import tpu as pltpu
from jax.sharding import Mesh
from jax.sharding import PartitionSpec as P

GROUP = 256
TILE = 512
PAD = 16
F32 = jnp.float32
BF16 = jnp.bfloat16
PAIR = [(0, 1), (1, 0)]


def ring(size, step):
    return [(i, (i + step) % size) for i in range(size)]


def dct_rows(band, length):
    index = band.astype(F32)[:, None]
    cells = jnp.arange(length, dtype=F32)[None, :]
    factor = jnp.where(band == 0, math.sqrt(1.0 / length), math.sqrt(2.0 / length)).astype(F32)
    return factor[:, None] * jnp.cos(math.pi * (cells + 0.5) * index / length)


def split(value):
    high = value.astype(BF16)
    return high, (value - high.astype(F32)).astype(BF16)


def dot(a, b, dims):
    return lax.dot_general(a, b, ((dims[:1], dims[1:]), ((), ())), preferred_element_type=F32)


def decode(coefficients, stacked):
    high, low = split(coefficients)
    return dot(jnp.concatenate([high, low, high], axis=0), stacked, (0, 0))


def encode(pair, values, band):
    both = dot(pair, values, (1, 1))
    return both[:band] + both[band:]


def block(index, size):
    return slice(index * size, (index + 1) * size)


def load_kernel(band, place, grad_out, momentum, pair, x_rows, coded, kept, own, grad_in, total, momentum_in, sems):
    blocks = grad_in.shape[1] // GROUP
    halves = [block(h, grad_in.shape[0] // 2) for h in range(2)]
    ends = [(momentum.at[0], momentum_in)] + [(grad_out.at[h], grad_in.at[h]) for h in halves] + [(x_rows, own)]
    copies = [pltpu.make_async_copy(*pair, sems.at[c]) for c, pair in enumerate(ends)]
    for copy in copies:
        copy.start()
    copies[0].wait()
    for b in range(blocks):
        kept[block(b, band), :] = 0.9 * encode(pair[...], momentum_in[:, block(b, GROUP)], band)
    for copy, half in zip(copies[1:3], halves):
        copy.wait()
        for b in range(blocks):
            high, low = split(encode(pair[...], grad_in[half, block(b, GROUP)], band))
            coded[block(b, band), half] = high
            coded[block(blocks + b, band), half] = low
    copies[3].wait()
    for i in range(total.shape[0] // TILE):
        rows = block(i, TILE)
        kept[:, rows] = kept[:, rows] + code_sum(place, [[own]], coded, rows)
        for w in range(total.shape[1] // TILE):
            wide = block(w, TILE)
            start = 0.9 * momentum_in[rows, wide].astype(F32)
            total[rows, wide] = start + grad_sum(place, [[own]], grad_in, rows, wide)


def tokens_of(place, count):
    return pl.ds(pl.multiple_of(place * count, count), count)


def chunks(groups, refs):
    taken, out = 0, []
    for count in groups:
        out.append(refs[taken : taken + count])
        taken += count
    return out, refs[taken:]


def take(pieces, columns):
    parts = [piece[:, columns] for piece in pieces]
    return parts[0] if len(parts) == 1 else jnp.concatenate(parts, axis=0)


def code_sum(places, xs, coded, columns):
    value = 0.0
    half = coded.shape[0] // 2
    for s, pieces in enumerate(xs):
        x = take(pieces, columns)
        value = value + dot(coded[:, tokens_of(places[s], x.shape[0])], x, (1, 0))
    return value[:half] + value[half:]


def grad_sum(places, xs, grad_in, rows, columns):
    value = 0.0
    for s, pieces in enumerate(xs):
        x = take(pieces, rows)
        value = value + dot(x, grad_in[tokens_of(places[s], x.shape[0]), columns], (0, 0))
    return value


def add_kernel(groups, span, places, *refs):
    xs, refs = chunks(groups, refs)
    grad_in, base = refs[:2]
    total, staged, sems = refs[-3:]
    copies = []
    for w in range(total.shape[1] // TILE):
        wide = block(w, TILE)
        staged[:, wide] = base[span, wide] + grad_sum(places, xs, grad_in, span, wide)
        copies.append(pltpu.make_async_copy(staged.at[:, wide], total.at[span, wide], sems.at[w]))
        copies[-1].start()
    for copy in copies:
        copy.wait()


def tally_kernel(groups, places, *refs):
    xs, refs = chunks(groups, refs)
    coded, kept, kept_out = refs
    half = kept.shape[1] // 2
    for i in range(2):
        rows = block(i, half)
        kept_out[:, rows] = kept[:, rows] + code_sum(places, xs, coded, rows)


def code_kernel(groups, places, core, *refs):
    xs, refs = chunks(groups, refs)
    coded, kept, kept_out, mine, other = refs
    rows = kept.shape[1] // 2

    def half(index, out):
        columns = pl.ds(pl.multiple_of(index * rows, rows), rows)
        value = kept[:, columns] + code_sum(places, xs, coded, columns)
        kept_out[:, columns] = value
        for t in range(rows // 128):
            out[block(t, value.shape[0]), :] = value[:, block(t, 128)]

    half(1 - core[0], other)
    half(core[0], mine)


def fresh_kernel(groups, band, places, *refs):
    count = sum(groups)
    xs, refs = refs[:count], refs[count:]
    grad_out, total, kept, stacked, fresh, x_in, g_in, total_in, kept_in, staged, sems, out_sems = refs
    rows, columns = total.shape
    steps, wides = rows // TILE, columns // TILE
    tokens = x_in.shape[0] // len(groups)
    ends = []
    ready = [[0] * wides for _ in range(steps)]
    for i in range(steps):
        span, start = block(i, TILE), 0
        for x in xs:
            ends.append((x.at[:, span], x_in.at[start : start + x.shape[0], span]))
            start += x.shape[0]
        for w in range(wides):
            wide = block(w, TILE)
            for s in range(len(groups) if i == 0 else 0):
                ends.append((grad_out.at[tokens_of(places[s], tokens), wide], g_in.at[block(s, tokens), wide]))
            ends.append((total.at[span, wide], total_in.at[span, wide]))
            if w == 0:
                ends.append((kept.at[:, span], kept_in.at[:, span]))
            ready[i][w] = len(ends)
    copies = [pltpu.make_async_copy(*pair, sems.at[i]) for i, pair in enumerate(ends)]
    for copy in copies:
        copy.start()
    waited, outs = 0, []
    for i in range(steps):
        span = block(i, TILE)
        for w in range(wides):
            for copy in copies[waited : ready[i][w]]:
                copy.wait()
            waited = ready[i][w]
            for b in range(w * TILE // GROUP, (w + 1) * TILE // GROUP):
                cols = block(b, GROUP)
                value = total_in[span, cols] + dot(x_in[:, span], g_in[:, cols], (0, 0))
                value = value - decode(kept_in[block(b, band), span], stacked[...])
                staged[span, cols] = value.astype(BF16)
        outs.append(pltpu.make_async_copy(staged.at[span], fresh.at[0, span], out_sems.at[i]))
        outs[-1].start()
    for out in outs:
        out.wait()


def join_kernel(mine, other, kept, out, kept_out, staged, sems):
    save = pltpu.make_async_copy(kept, kept_out, sems.at[0])
    staged[...] = mine[...] + other[...]
    give = pltpu.make_async_copy(staged, out, sems.at[1])
    give.start()
    save.start()
    give.wait()
    save.wait()


def part_kernel(chips, parts, spread):
    rows = parts.shape[0] // chips
    value = parts[:rows, :]
    for i in range(1, chips):
        value = value + parts[block(i, rows), :]
    largest = jnp.maximum(jnp.max(jnp.abs(value), axis=0, keepdims=True), 2.0**-100)
    power = jnp.ceil(jnp.log2(largest))
    level = jnp.round(value * jnp.exp2(15.0 - power))
    level = jnp.clip(level, -32767.0, 32767.0).astype(jnp.int32).astype(jnp.int16)
    power = jnp.broadcast_to(power, (PAD, value.shape[1])).astype(jnp.int32).astype(jnp.int16)
    for i in range(chips):
        start = i * (rows + PAD)
        spread[start : start + rows, :] = level
        spread[start + rows : start + rows + PAD, :] = power


def update_kernel(band, chips, where, whole, stacked, *refs):
    update, staged, sems = refs[-3:]
    rows = whole.shape[0] // chips - PAD
    values = []
    for i in range(chips):
        start = i * (rows + PAD)
        level = whole[start : start + rows, :].astype(jnp.int32).astype(F32)
        power = whole[start + rows : start + rows + PAD, :].astype(jnp.int32).astype(F32)[:1]
        values.append(level * jnp.exp2(power - 15.0))
    value = jnp.concatenate(values, axis=0)
    tiles = staged.shape[0] // 128
    kept = value.shape[0] // tiles
    span = pl.ds(pl.multiple_of(where[0] * staged.shape[0], staged.shape[0]), staged.shape[0])
    outs = []
    for w in range(staged.shape[1] // TILE):
        for b in range(w * TILE // GROUP, (w + 1) * TILE // GROUP):
            parts = [value[t * kept + b * band : t * kept + (b + 1) * band] for t in range(tiles)]
            staged[:, block(b, GROUP)] = decode(jnp.concatenate(parts, axis=1), stacked[...]).astype(BF16)
        wide = block(w, TILE)
        outs.append(pltpu.make_async_copy(staged.at[:, wide], update.at[span, wide], sems.at[w]))
        outs[-1].start()
    for out in outs:
        out.wait()


VMEM = pl.BlockSpec(memory_space=pltpu.VMEM)
SMEM = pl.BlockSpec(memory_space=pltpu.SMEM)
ANY = pl.BlockSpec(memory_space=pl.ANY)
HBM = pl.BlockSpec(memory_space=pltpu.HBM)


def params(mib):
    return pltpu.CompilerParams(vmem_limit_bytes=mib << 20)


def held(value):
    return pltpu.with_memory_space_constraint(value, pltpu.VMEM)


def far(value):
    return pltpu.with_memory_space_constraint(value, pltpu.HBM)


def estimate(flops, size):
    return pl.CostEstimate(flops=flops, bytes_accessed=size, transcendentals=0)


def load(place, grad_out, momentum, pair, x_rows, band):
    tokens, columns = grad_out.shape
    rows = momentum.shape[1]
    kept = columns // GROUP * band
    return pl.pallas_call(
        functools.partial(load_kernel, band),
        in_specs=[SMEM, ANY, ANY, VMEM, ANY],
        out_specs=[VMEM] * 5,
        out_shape=[
            pltpu.VMEM((2 * kept, tokens), BF16),
            pltpu.VMEM((kept, rows), F32),
            pltpu.VMEM(x_rows.shape, BF16),
            pltpu.VMEM(grad_out.shape, BF16),
            pltpu.VMEM((rows, columns), F32),
        ],
        scratch_shapes=[pltpu.VMEM((rows, columns), BF16), pltpu.SemaphoreType.DMA((4,))],
        compiler_params=params(16),
        cost_estimate=estimate(2 * columns * (tokens + rows) * 256, 2 * columns * (tokens + rows)),
        name="load",
    )(place, far(grad_out), far(momentum), pair, far(x_rows))


def flat(chunks):
    pieces = [piece for chunk in chunks for piece in chunk]
    return tuple(map(len, chunks)), pieces, len(pieces), sum(piece.shape[0] for piece in pieces)


def add(span, places, xs, grad_in, base, total=None):
    groups, xs, count, tokens = flat(xs)
    shape = base.shape
    rows = span.stop - span.start
    others = [] if total is None else [far(total)]
    return pl.pallas_call(
        functools.partial(add_kernel, groups, span),
        in_specs=[SMEM] + [VMEM] * (count + 2) + [ANY] * len(others),
        out_specs=ANY,
        out_shape=pltpu.HBM(shape, F32),
        input_output_aliases={count + 3: 0} if others else {},
        scratch_shapes=[pltpu.VMEM((rows, shape[1]), F32), pltpu.SemaphoreType.DMA((shape[1] // TILE,))],
        compiler_params=params(16),
        cost_estimate=estimate(2 * tokens * rows * shape[1], rows * shape[1] * 4),
        name="add",
    )(places, *[held(x) for x in xs], held(grad_in), held(base), *others)


def tally(places, xs, coded, kept):
    groups, xs, count, tokens = flat(xs)
    size, rows = kept.shape
    return pl.pallas_call(
        functools.partial(tally_kernel, groups),
        in_specs=[SMEM] + [VMEM] * (count + 2),
        out_specs=VMEM,
        out_shape=pltpu.VMEM(kept.shape, F32),
        compiler_params=params(16),
        cost_estimate=estimate(2 * tokens * rows * size * 2, 0),
        name="tally",
    )(places, *[held(x) for x in xs], held(coded), held(kept))


def code(places, core, xs, coded, kept):
    groups, xs, count, tokens = flat(xs)
    size, rows = kept.shape
    out = jax.ShapeDtypeStruct((size * rows // 256, 128), F32)
    return pl.pallas_call(
        functools.partial(code_kernel, groups),
        in_specs=[SMEM, SMEM] + [VMEM] * (count + 2),
        out_specs=[VMEM] * 3,
        out_shape=[pltpu.VMEM(kept.shape, F32), pltpu.VMEM(out.shape, F32), pltpu.VMEM(out.shape, F32)],
        compiler_params=params(16),
        cost_estimate=estimate(2 * tokens * rows * size * 2, 0),
        name="code",
    )(places, core, *[held(x) for x in xs], held(coded), held(kept))


def finish(places, xs, grad_out, total, kept, stacked, band):
    groups, xs, count, tokens = flat(xs)
    rows, columns = total.shape
    steps, wides = rows // TILE, columns // TILE
    loads = (count + 1) * steps + wides * (len(groups) + steps)
    return pl.pallas_call(
        functools.partial(fresh_kernel, groups, band),
        in_specs=[SMEM] + [ANY] * (count + 3) + [VMEM],
        out_specs=ANY,
        out_shape=jax.ShapeDtypeStruct((1, rows, columns), BF16),
        scratch_shapes=[
            pltpu.VMEM((tokens, rows), BF16),
            pltpu.VMEM((tokens, columns), BF16),
            pltpu.VMEM(total.shape, F32),
            pltpu.VMEM(kept.shape, F32),
            pltpu.VMEM((rows, columns), BF16),
            pltpu.SemaphoreType.DMA((loads,)),
            pltpu.SemaphoreType.DMA((steps,)),
        ],
        compiler_params=params(24),
        cost_estimate=estimate(4 * tokens * rows * columns, rows * columns * 6),
        name="finish",
    )(places, *map(far, xs), far(grad_out), far(total), far(kept), stacked)


def join(mine, other, kept):
    return pl.pallas_call(
        join_kernel,
        in_specs=[VMEM] * 3,
        out_specs=[ANY] * 2,
        out_shape=[pltpu.HBM(mine.shape, F32), pltpu.HBM(kept.shape, F32)],
        scratch_shapes=[pltpu.VMEM(mine.shape, F32), pltpu.SemaphoreType.DMA((2,))],
        compiler_params=params(4),
        name="join",
    )(held(mine), held(other), held(kept))


def sum_parts(parts, chips):
    return pl.pallas_call(
        functools.partial(part_kernel, chips),
        in_specs=[VMEM],
        out_specs=VMEM,
        out_shape=pltpu.VMEM((parts.shape[0] + chips * PAD, parts.shape[1]), jnp.int16),
        compiler_params=params(16),
        name="sum_parts",
    )(held(parts))


def make_update(where, whole, stacked, band, rows, columns, update=None):
    others = [] if update is None else [update]
    return pl.pallas_call(
        functools.partial(update_kernel, band, 16),
        in_specs=[SMEM, VMEM, VMEM] + [ANY] * len(others),
        out_specs=ANY,
        out_shape=jax.ShapeDtypeStruct((rows, columns), BF16),
        input_output_aliases={3: 0} if others else {},
        scratch_shapes=[pltpu.VMEM((rows // 2, columns), BF16), pltpu.SemaphoreType.DMA((columns // TILE,))],
        compiler_params=params(16),
        cost_estimate=estimate(rows * columns * 96, rows * columns),
        name="update",
    )(where, held(whole), held(stacked), *others)


def shards(x_rows, grad_out, momentum, band_index):
    band = band_index.shape[0]
    basis = dct_rows(band_index, GROUP)
    rounded = lax.reduce_precision(basis, 8, 7)
    high, low = rounded.astype(BF16), (basis - rounded).astype(BF16)
    pair = jnp.concatenate([high, low], axis=0)
    stacked = jnp.concatenate([high, high, low], axis=0)

    y, xl = lax.axis_index("y"), lax.axis_index("xl")
    core = lax.axis_index("core").astype(jnp.int32).reshape(1)

    def places(*steps):
        return jnp.stack([((y + dy) % 4) * 2 + (xl + dx) % 2 for dy, dx in steps]).astype(jnp.int32)

    def across(v):
        return lax.ppermute(v, "xl", PAIR)

    def from_above(v):
        return lax.ppermute(v, "y", ring(4, -1))

    def from_below(v):
        return lax.ppermute(v, "y", ring(4, 1))

    first = places((0, 0))
    near = places((0, 1), (1, 0), (3, 0))
    middle = places((1, 1), (3, 1), (2, 0))
    last = places((2, 1))
    ends = places((1, 1), (3, 1), (2, 0), (2, 1))
    apart = 1 - core
    pair, stacked, first, near, middle, last, ends, core, apart = lax.optimization_barrier(
        (pair, stacked, first, near, middle, last, ends, core, apart)
    )
    with jax.named_scope("gather_near"):
        yp, xn, ym = from_above(x_rows), across(x_rows), from_below(x_rows)
        loaded = load(first, grad_out, momentum, pair, x_rows, band)
        yp, (coded, kept, own, grad_in, base) = lax.optimization_barrier((yp, loaded))
        xn, ym = lax.optimization_barrier((xn, ym))
    half = yp.shape[0] // 2
    with jax.named_scope("gather_middle"):
        y2 = [from_above(yp[:half])]
        xyp = across(yp)
        y2.append(from_above(yp[half:]))
        xym = [from_below(xn[half:])]
        xym.insert(0, from_below(xn[:half]))
    rows = momentum.shape[1]
    close = [[xn], [yp], [ym]]
    total = add(slice(0, rows // 2), near, close, grad_in, base)
    y2[0], xym[1], total = lax.optimization_barrier((y2[0], xym[1], total))
    with jax.named_scope("gather_far"):
        xy2 = [across(y2[0]), from_below(xym[1])]
    total = add(slice(rows // 2, rows), near, close, grad_in, base, total)
    kept = tally(near, close, coded, kept)
    kept = tally(middle, [[xyp], xym, y2], coded, kept)
    kept, total = lax.optimization_barrier((kept, total))
    kept, mine, other = code(last, core, [xy2], coded, kept)
    with jax.named_scope("sum_core"):
        mine, kept = join(mine, lax.ppermute(other, "core", PAIR), kept)
    with jax.named_scope("sum_chips"):
        parts = lax.all_to_all(mine, ("z", "xh"), 0, 0, tiled=True)
    fresh = finish(ends, [[xyp], xym, y2, xy2], grad_out, total, kept, stacked, band)
    parts, fresh = lax.optimization_barrier((parts, fresh))
    with jax.named_scope("spread_chips"):
        whole = lax.all_to_all(sum_parts(parts, 16), ("z", "xh"), 0, 0, tiled=True)
    with jax.named_scope("spread_core"):
        other = lax.ppermute(whole, "core", PAIR)
    update = make_update(core, whole, stacked, band, rows, grad_out.shape[1])
    return fresh, make_update(apart, other, stacked, band, rows, grad_out.shape[1], update)


def solution(mesh):
    fine = Mesh(mesh.devices.reshape(8, 2, 2, 4, 2), ("z", "xh", "core", "y", "xl"))
    rep, col = ("z", "xh", "core"), ("y", "xl")
    return jax.shard_map(
        shards,
        mesh=fine,
        in_specs=(P(rep + col, None), P(rep, col), P(rep, None, col), P()),
        out_specs=(P(rep, None, col), P(None, col)),
        check_vma=False,
    )
```

```python
import functools
import math

import jax
import jax.numpy as jnp
from jax import lax
from jax.experimental import pallas as pl
from jax.experimental.pallas import tpu as pltpu
from jax.sharding import Mesh
from jax.sharding import PartitionSpec as P

GROUP = 256
TILE = 512
PAD = 16
F32 = jnp.float32
BF16 = jnp.bfloat16
PAIR = [(0, 1), (1, 0)]


def ring(size, step):
    return [(i, (i + step) % size) for i in range(size)]


def dct_rows(band, length):
    index = band.astype(F32)[:, None]
    cells = jnp.arange(length, dtype=F32)[None, :]
    factor = jnp.where(band == 0, math.sqrt(1.0 / length), math.sqrt(2.0 / length)).astype(F32)
    return factor[:, None] * jnp.cos(math.pi * (cells + 0.5) * index / length)


def split(value):
    high = value.astype(BF16)
    return high, (value - high.astype(F32)).astype(BF16)


def dot(a, b, dims):
    return lax.dot_general(a, b, ((dims[:1], dims[1:]), ((), ())), preferred_element_type=F32)


def decode(coefficients, stacked):
    high, low = split(coefficients)
    return dot(jnp.concatenate([high, low, high], axis=0), stacked, (0, 0))


def encode(pair, values, band):
    both = dot(pair, values, (1, 1))
    return both[:band] + both[band:]


def block(index, size):
    return slice(index * size, (index + 1) * size)


def load_kernel(band, place, grad_out, momentum, pair, x_rows, coded, kept, own, grad_in, total, momentum_in, sems):
    blocks = grad_in.shape[1] // GROUP
    halves = [block(h, grad_in.shape[0] // 2) for h in range(2)]
    ends = [(momentum.at[0], momentum_in)] + [(grad_out.at[h], grad_in.at[h]) for h in halves] + [(x_rows, own)]
    copies = [pltpu.make_async_copy(*pair, sems.at[c]) for c, pair in enumerate(ends)]
    for copy in copies:
        copy.start()
    copies[0].wait()
    for b in range(blocks):
        kept[block(b, band), :] = 0.9 * encode(pair[...], momentum_in[:, block(b, GROUP)], band)
    for copy, half in zip(copies[1:3], halves):
        copy.wait()
        for b in range(blocks):
            high, low = split(encode(pair[...], grad_in[half, block(b, GROUP)], band))
            coded[block(b, band), half] = high
            coded[block(blocks + b, band), half] = low
    copies[3].wait()
    for i in range(total.shape[0] // TILE):
        rows = block(i, TILE)
        kept[:, rows] = kept[:, rows] + code_sum(place, [[own]], coded, rows)
        for w in range(total.shape[1] // TILE):
            wide = block(w, TILE)
            start = 0.9 * momentum_in[rows, wide].astype(F32)
            total[rows, wide] = start + grad_sum(place, [[own]], grad_in, rows, wide)


def tokens_of(place, count):
    return pl.ds(pl.multiple_of(place * count, count), count)


def chunks(groups, refs):
    taken, out = 0, []
    for count in groups:
        out.append(refs[taken : taken + count])
        taken += count
    return out, refs[taken:]


def take(pieces, columns):
    parts = [piece[:, columns] for piece in pieces]
    return parts[0] if len(parts) == 1 else jnp.concatenate(parts, axis=0)


def code_sum(places, xs, coded, columns):
    value = 0.0
    half = coded.shape[0] // 2
    for s, pieces in enumerate(xs):
        x = take(pieces, columns)
        value = value + dot(coded[:, tokens_of(places[s], x.shape[0])], x, (1, 0))
    return value[:half] + value[half:]


def grad_sum(places, xs, grad_in, rows, columns):
    value = 0.0
    for s, pieces in enumerate(xs):
        x = take(pieces, rows)
        value = value + dot(x, grad_in[tokens_of(places[s], x.shape[0]), columns], (0, 0))
    return value


def add_kernel(groups, span, places, *refs):
    xs, refs = chunks(groups, refs)
    grad_in, base = refs[:2]
    total, staged, sems = refs[-3:]
    copies = []
    for w in range(total.shape[1] // TILE):
        wide = block(w, TILE)
        staged[:, wide] = base[span, wide] + grad_sum(places, xs, grad_in, span, wide)
        copies.append(pltpu.make_async_copy(staged.at[:, wide], total.at[span, wide], sems.at[w]))
        copies[-1].start()
    for copy in copies:
        copy.wait()


def tally_kernel(groups, places, *refs):
    xs, refs = chunks(groups, refs)
    coded, kept, kept_out = refs
    half = kept.shape[1] // 2
    for i in range(2):
        rows = block(i, half)
        kept_out[:, rows] = kept[:, rows] + code_sum(places, xs, coded, rows)


def code_kernel(groups, places, core, *refs):
    xs, refs = chunks(groups, refs)
    coded, kept, kept_out, mine, other = refs
    rows = kept.shape[1] // 2

    def half(index, out):
        columns = pl.ds(pl.multiple_of(index * rows, rows), rows)
        value = kept[:, columns] + code_sum(places, xs, coded, columns)
        kept_out[:, columns] = value
        for t in range(rows // 128):
            out[block(t, value.shape[0]), :] = value[:, block(t, 128)]

    half(1 - core[0], other)
    half(core[0], mine)


def fresh_kernel(groups, band, places, *refs):
    count = sum(groups)
    xs, refs = refs[:count], refs[count:]
    grad_out, total, kept, stacked, fresh, x_in, g_in, total_in, kept_in, staged, sems, out_sems = refs
    rows, columns = total.shape
    steps, wides = rows // TILE, columns // TILE
    tokens = x_in.shape[0] // len(groups)
    ends = []
    ready = [[0] * wides for _ in range(steps)]
    for i in range(steps):
        span, start = block(i, TILE), 0
        for x in xs:
            ends.append((x.at[:, span], x_in.at[start : start + x.shape[0], span]))
            start += x.shape[0]
        for w in range(wides):
            wide = block(w, TILE)
            for s in range(len(groups) if i == 0 else 0):
                ends.append((grad_out.at[tokens_of(places[s], tokens), wide], g_in.at[block(s, tokens), wide]))
            ends.append((total.at[span, wide], total_in.at[span, wide]))
            if w == 0:
                ends.append((kept.at[:, span], kept_in.at[:, span]))
            ready[i][w] = len(ends)
    copies = [pltpu.make_async_copy(*pair, sems.at[i]) for i, pair in enumerate(ends)]
    for copy in copies:
        copy.start()
    waited, outs = 0, []
    for i in range(steps):
        span = block(i, TILE)
        for w in range(wides):
            for copy in copies[waited : ready[i][w]]:
                copy.wait()
            waited = ready[i][w]
            for b in range(w * TILE // GROUP, (w + 1) * TILE // GROUP):
                cols = block(b, GROUP)
                value = total_in[span, cols] + dot(x_in[:, span], g_in[:, cols], (0, 0))
                value = value - decode(kept_in[block(b, band), span], stacked[...])
                staged[span, cols] = value.astype(BF16)
        outs.append(pltpu.make_async_copy(staged.at[span], fresh.at[0, span], out_sems.at[i]))
        outs[-1].start()
    for out in outs:
        out.wait()


def save_kernel(kept, kept_out, sem):
    copy = pltpu.make_async_copy(kept, kept_out, sem)
    copy.start()
    copy.wait()


def join_kernel(mine, other, out, staged, sems):
    halves = [block(h, mine.shape[0] // 2) for h in range(2)]
    copies = []
    for h, half in enumerate(halves):
        staged[half, :] = mine[half, :] + other[half, :]
        copies.append(pltpu.make_async_copy(staged.at[half], out.at[half], sems.at[h]))
        copies[-1].start()
    for copy in copies:
        copy.wait()


def part_kernel(chips, parts, spread):
    rows = parts.shape[0] // chips
    value = parts[:rows, :]
    for i in range(1, chips):
        value = value + parts[block(i, rows), :]
    largest = jnp.maximum(jnp.max(jnp.abs(value), axis=0, keepdims=True), 2.0**-100)
    power = jnp.ceil(jnp.log2(largest))
    level = jnp.round(value * jnp.exp2(15.0 - power))
    level = jnp.clip(level, -32767.0, 32767.0).astype(jnp.int32).astype(jnp.int16)
    power = jnp.broadcast_to(power, (PAD, value.shape[1])).astype(jnp.int32).astype(jnp.int16)
    for i in range(chips):
        start = i * (rows + PAD)
        spread[start : start + rows, :] = level
        spread[start + rows : start + rows + PAD, :] = power


def update_kernel(band, chips, where, whole, stacked, *refs):
    update, staged, sems = refs[-3:]
    rows = whole.shape[0] // chips - PAD
    values = []
    for i in range(chips):
        start = i * (rows + PAD)
        level = whole[start : start + rows, :].astype(jnp.int32).astype(F32)
        power = whole[start + rows : start + rows + PAD, :].astype(jnp.int32).astype(F32)[:1]
        values.append(level * jnp.exp2(power - 15.0))
    value = jnp.concatenate(values, axis=0)
    tiles = staged.shape[0] // 128
    kept = value.shape[0] // tiles
    span = pl.ds(pl.multiple_of(where[0] * staged.shape[0], staged.shape[0]), staged.shape[0])
    outs = []
    for w in range(staged.shape[1] // TILE):
        for b in range(w * TILE // GROUP, (w + 1) * TILE // GROUP):
            parts = [value[t * kept + b * band : t * kept + (b + 1) * band] for t in range(tiles)]
            staged[:, block(b, GROUP)] = decode(jnp.concatenate(parts, axis=1), stacked[...]).astype(BF16)
        wide = block(w, TILE)
        outs.append(pltpu.make_async_copy(staged.at[:, wide], update.at[span, wide], sems.at[w]))
        outs[-1].start()
    for out in outs:
        out.wait()


VMEM = pl.BlockSpec(memory_space=pltpu.VMEM)
SMEM = pl.BlockSpec(memory_space=pltpu.SMEM)
ANY = pl.BlockSpec(memory_space=pl.ANY)
HBM = pl.BlockSpec(memory_space=pltpu.HBM)


def params(mib):
    return pltpu.CompilerParams(vmem_limit_bytes=mib << 20)


def held(value):
    return pltpu.with_memory_space_constraint(value, pltpu.VMEM)


def far(value):
    return pltpu.with_memory_space_constraint(value, pltpu.HBM)


def estimate(flops, size):
    return pl.CostEstimate(flops=flops, bytes_accessed=size, transcendentals=0)


def load(place, grad_out, momentum, pair, x_rows, band):
    tokens, columns = grad_out.shape
    rows = momentum.shape[1]
    kept = columns // GROUP * band
    return pl.pallas_call(
        functools.partial(load_kernel, band),
        in_specs=[SMEM, ANY, ANY, VMEM, ANY],
        out_specs=[VMEM] * 5,
        out_shape=[
            pltpu.VMEM((2 * kept, tokens), BF16),
            pltpu.VMEM((kept, rows), F32),
            pltpu.VMEM(x_rows.shape, BF16),
            pltpu.VMEM(grad_out.shape, BF16),
            pltpu.VMEM((rows, columns), F32),
        ],
        scratch_shapes=[pltpu.VMEM((rows, columns), BF16), pltpu.SemaphoreType.DMA((4,))],
        compiler_params=params(16),
        cost_estimate=estimate(2 * columns * (tokens + rows) * 256, 2 * columns * (tokens + rows)),
        name="load",
    )(place, far(grad_out), far(momentum), pair, far(x_rows))


def flat(chunks):
    pieces = [piece for chunk in chunks for piece in chunk]
    return tuple(map(len, chunks)), pieces, len(pieces), sum(piece.shape[0] for piece in pieces)


def add(span, places, xs, grad_in, base, total=None):
    groups, xs, count, tokens = flat(xs)
    shape = base.shape
    rows = span.stop - span.start
    others = [] if total is None else [far(total)]
    return pl.pallas_call(
        functools.partial(add_kernel, groups, span),
        in_specs=[SMEM] + [VMEM] * (count + 2) + [ANY] * len(others),
        out_specs=ANY,
        out_shape=pltpu.HBM(shape, F32),
        input_output_aliases={count + 3: 0} if others else {},
        scratch_shapes=[pltpu.VMEM((rows, shape[1]), F32), pltpu.SemaphoreType.DMA((shape[1] // TILE,))],
        compiler_params=params(16),
        cost_estimate=estimate(2 * tokens * rows * shape[1], rows * shape[1] * 4),
        name="add",
    )(places, *[held(x) for x in xs], held(grad_in), held(base), *others)


def tally(places, xs, coded, kept):
    groups, xs, count, tokens = flat(xs)
    size, rows = kept.shape
    return pl.pallas_call(
        functools.partial(tally_kernel, groups),
        in_specs=[SMEM] + [VMEM] * (count + 2),
        out_specs=VMEM,
        out_shape=pltpu.VMEM(kept.shape, F32),
        compiler_params=params(16),
        cost_estimate=estimate(2 * tokens * rows * size * 2, 0),
        name="tally",
    )(places, *[held(x) for x in xs], held(coded), held(kept))


def code(places, core, xs, coded, kept):
    groups, xs, count, tokens = flat(xs)
    size, rows = kept.shape
    out = jax.ShapeDtypeStruct((size * rows // 256, 128), F32)
    return pl.pallas_call(
        functools.partial(code_kernel, groups),
        in_specs=[SMEM, SMEM] + [VMEM] * (count + 2),
        out_specs=[VMEM] * 3,
        out_shape=[pltpu.VMEM(kept.shape, F32), pltpu.VMEM(out.shape, F32), pltpu.VMEM(out.shape, F32)],
        compiler_params=params(16),
        cost_estimate=estimate(2 * tokens * rows * size * 2, 0),
        name="code",
    )(places, core, *[held(x) for x in xs], held(coded), held(kept))


def finish(places, xs, grad_out, total, kept, stacked, band):
    groups, xs, count, tokens = flat(xs)
    rows, columns = total.shape
    steps, wides = rows // TILE, columns // TILE
    loads = (count + 1) * steps + wides * (len(groups) + steps)
    return pl.pallas_call(
        functools.partial(fresh_kernel, groups, band),
        in_specs=[SMEM] + [ANY] * (count + 3) + [VMEM],
        out_specs=ANY,
        out_shape=jax.ShapeDtypeStruct((1, rows, columns), BF16),
        scratch_shapes=[
            pltpu.VMEM((tokens, rows), BF16),
            pltpu.VMEM((tokens, columns), BF16),
            pltpu.VMEM(total.shape, F32),
            pltpu.VMEM(kept.shape, F32),
            pltpu.VMEM((rows, columns), BF16),
            pltpu.SemaphoreType.DMA((loads,)),
            pltpu.SemaphoreType.DMA((steps,)),
        ],
        compiler_params=params(24),
        cost_estimate=estimate(4 * tokens * rows * columns, rows * columns * 6),
        name="finish",
    )(places, *map(far, xs), far(grad_out), far(total), far(kept), stacked)


def save(kept):
    return pl.pallas_call(
        save_kernel,
        in_specs=[VMEM],
        out_specs=ANY,
        out_shape=pltpu.HBM(kept.shape, F32),
        scratch_shapes=[pltpu.SemaphoreType.DMA],
        compiler_params=params(4),
        cost_estimate=estimate(0, kept.size * 4),
        name="save",
    )(held(kept))


def join(mine, other):
    return pl.pallas_call(
        join_kernel,
        in_specs=[VMEM] * 2,
        out_specs=ANY,
        out_shape=pltpu.HBM(mine.shape, F32),
        scratch_shapes=[pltpu.VMEM(mine.shape, F32), pltpu.SemaphoreType.DMA((2,))],
        compiler_params=params(4),
        name="join",
    )(held(mine), held(other))


def sum_parts(parts, chips):
    return pl.pallas_call(
        functools.partial(part_kernel, chips),
        in_specs=[VMEM],
        out_specs=VMEM,
        out_shape=pltpu.VMEM((parts.shape[0] + chips * PAD, parts.shape[1]), jnp.int16),
        compiler_params=params(16),
        name="sum_parts",
    )(held(parts))


def make_update(where, whole, stacked, band, rows, columns, update=None):
    others = [] if update is None else [update]
    return pl.pallas_call(
        functools.partial(update_kernel, band, 16),
        in_specs=[SMEM, VMEM, VMEM] + [ANY] * len(others),
        out_specs=ANY,
        out_shape=jax.ShapeDtypeStruct((rows, columns), BF16),
        input_output_aliases={3: 0} if others else {},
        scratch_shapes=[pltpu.VMEM((rows // 2, columns), BF16), pltpu.SemaphoreType.DMA((columns // TILE,))],
        compiler_params=params(16),
        cost_estimate=estimate(rows * columns * 96, rows * columns),
        name="update",
    )(where, held(whole), held(stacked), *others)


def shards(x_rows, grad_out, momentum, band_index):
    band = band_index.shape[0]
    basis = dct_rows(band_index, GROUP)
    rounded = lax.reduce_precision(basis, 8, 7)
    high, low = rounded.astype(BF16), (basis - rounded).astype(BF16)
    pair = jnp.concatenate([high, low], axis=0)
    stacked = jnp.concatenate([high, high, low], axis=0)

    y, xl = lax.axis_index("y"), lax.axis_index("xl")
    core = lax.axis_index("core").astype(jnp.int32).reshape(1)

    def places(*steps):
        return jnp.stack([((y + dy) % 4) * 2 + (xl + dx) % 2 for dy, dx in steps]).astype(jnp.int32)

    def across(v):
        return lax.ppermute(v, "xl", PAIR)

    def from_above(v):
        return lax.ppermute(v, "y", ring(4, -1))

    def from_below(v):
        return lax.ppermute(v, "y", ring(4, 1))

    first = places((0, 0))
    near = places((0, 1), (1, 0), (3, 0))
    middle = places((1, 1), (3, 1), (2, 0))
    last = places((2, 1))
    ends = places((1, 1), (3, 1), (2, 0), (2, 1))
    apart = 1 - core
    pair, stacked, first, near, middle, last, ends, core, apart = lax.optimization_barrier(
        (pair, stacked, first, near, middle, last, ends, core, apart)
    )
    with jax.named_scope("gather_near"):
        yp, xn, ym = from_above(x_rows), across(x_rows), from_below(x_rows)
        loaded = load(first, grad_out, momentum, pair, x_rows, band)
        yp, (coded, kept, own, grad_in, base) = lax.optimization_barrier((yp, loaded))
        xn, ym = lax.optimization_barrier((xn, ym))
    half = yp.shape[0] // 2
    with jax.named_scope("gather_middle"):
        y2 = [from_above(yp[:half])]
        xyp = across(yp)
        y2.append(from_above(yp[half:]))
        xym = [from_below(xn[half:])]
        xym.insert(0, from_below(xn[:half]))
    rows = momentum.shape[1]
    close = [[xn], [yp], [ym]]
    total = add(slice(0, rows // 2), near, close, grad_in, base)
    y2[0], total = lax.optimization_barrier((y2[0], total))
    with jax.named_scope("gather_far"):
        xy2 = [across(y2[0]), from_below(xym[1])]
    total = add(slice(rows // 2, rows), near, close, grad_in, base, total)
    kept = tally(near, close, coded, kept)
    kept = tally(middle, [[xyp], xym, y2], coded, kept)
    kept, total = lax.optimization_barrier((kept, total))
    kept, mine, other = code(last, core, [xy2], coded, kept)
    with jax.named_scope("sum_core"):
        other, kept = lax.optimization_barrier((lax.ppermute(other, "core", PAIR), save(kept)))
        mine = join(mine, other)
    with jax.named_scope("sum_chips"):
        parts = lax.all_to_all(mine, ("z", "xh"), 0, 0, tiled=True)
    fresh = finish(ends, [[xyp], xym, y2, xy2], grad_out, total, kept, stacked, band)
    parts, fresh = lax.optimization_barrier((parts, fresh))
    with jax.named_scope("spread_chips"):
        whole = lax.all_to_all(sum_parts(parts, 16), ("z", "xh"), 0, 0, tiled=True)
    with jax.named_scope("spread_core"):
        other = lax.ppermute(whole, "core", PAIR)
    update = make_update(core, whole, stacked, band, rows, grad_out.shape[1])
    return fresh, make_update(apart, other, stacked, band, rows, grad_out.shape[1], update)


def solution(mesh):
    fine = Mesh(mesh.devices.reshape(8, 2, 2, 4, 2), ("z", "xh", "core", "y", "xl"))
    rep, col = ("z", "xh", "core"), ("y", "xl")
    return jax.shard_map(
        shards,
        mesh=fine,
        in_specs=(P(rep + col, None), P(rep, col), P(rep, None, col), P()),
        out_specs=(P(rep, None, col), P(None, col)),
        check_vma=False,
    )
```

```python
import functools
import math

import jax
import jax.numpy as jnp
from jax import lax
from jax.experimental import pallas as pl
from jax.experimental.pallas import tpu as pltpu
from jax.sharding import Mesh
from jax.sharding import PartitionSpec as P

GROUP = 256
TILE = 512
PAD = 16
F32 = jnp.float32
BF16 = jnp.bfloat16
PAIR = [(0, 1), (1, 0)]


def ring(size, step):
    return [(i, (i + step) % size) for i in range(size)]


def dct_rows(band, length):
    index = band.astype(F32)[:, None]
    cells = jnp.arange(length, dtype=F32)[None, :]
    factor = jnp.where(band == 0, math.sqrt(1.0 / length), math.sqrt(2.0 / length)).astype(F32)
    return factor[:, None] * jnp.cos(math.pi * (cells + 0.5) * index / length)


def split(value):
    high = value.astype(BF16)
    return high, (value - high.astype(F32)).astype(BF16)


def dot(a, b, dims):
    return lax.dot_general(a, b, ((dims[:1], dims[1:]), ((), ())), preferred_element_type=F32)


def decode(coefficients, stacked):
    high, low = split(coefficients)
    return dot(jnp.concatenate([high, low, high], axis=0), stacked, (0, 0))


def encode(pair, values, band):
    both = dot(pair, values, (1, 1))
    return both[:band] + both[band:]


def block(index, size):
    return slice(index * size, (index + 1) * size)


def load_kernel(band, place, grad_out, momentum, pair, x_rows, coded, kept, own, grad_in, total, momentum_in, sems):
    blocks = grad_in.shape[1] // GROUP
    halves = [block(h, grad_in.shape[0] // 2) for h in range(2)]
    ends = [(momentum.at[0], momentum_in)] + [(grad_out.at[h], grad_in.at[h]) for h in halves] + [(x_rows, own)]
    copies = [pltpu.make_async_copy(*pair, sems.at[c]) for c, pair in enumerate(ends)]
    for copy in copies:
        copy.start()
    copies[0].wait()
    for b in range(blocks):
        kept[block(b, band), :] = 0.9 * encode(pair[...], momentum_in[:, block(b, GROUP)], band)
    for copy, half in zip(copies[1:3], halves):
        copy.wait()
        for b in range(blocks):
            high, low = split(encode(pair[...], grad_in[half, block(b, GROUP)], band))
            coded[block(b, band), half] = high
            coded[block(blocks + b, band), half] = low
    copies[3].wait()
    for i in range(total.shape[0] // TILE):
        rows = block(i, TILE)
        kept[:, rows] = kept[:, rows] + code_sum(place, [[own]], coded, rows)
        for w in range(total.shape[1] // TILE):
            wide = block(w, TILE)
            start = 0.9 * momentum_in[rows, wide].astype(F32)
            total[rows, wide] = start + grad_sum(place, [[own]], grad_in, rows, wide)


def tokens_of(place, count):
    return pl.ds(pl.multiple_of(place * count, count), count)


def chunks(groups, refs):
    taken, out = 0, []
    for count in groups:
        out.append(refs[taken : taken + count])
        taken += count
    return out, refs[taken:]


def take(pieces, columns):
    parts = [piece[:, columns] for piece in pieces]
    return parts[0] if len(parts) == 1 else jnp.concatenate(parts, axis=0)


def code_sum(places, xs, coded, columns):
    value = 0.0
    half = coded.shape[0] // 2
    for s, pieces in enumerate(xs):
        x = take(pieces, columns)
        value = value + dot(coded[:, tokens_of(places[s], x.shape[0])], x, (1, 0))
    return value[:half] + value[half:]


def grad_sum(places, xs, grad_in, rows, columns):
    value = 0.0
    for s, pieces in enumerate(xs):
        x = take(pieces, rows)
        value = value + dot(x, grad_in[tokens_of(places[s], x.shape[0]), columns], (0, 0))
    return value


def add_kernel(groups, span, places, *refs):
    xs, refs = chunks(groups, refs)
    grad_in, base = refs[:2]
    total, staged, sems = refs[-3:]
    copies = []
    for w in range(total.shape[1] // TILE):
        wide = block(w, TILE)
        staged[:, wide] = base[span, wide] + grad_sum(places, xs, grad_in, span, wide)
        copies.append(pltpu.make_async_copy(staged.at[:, wide], total.at[span, wide], sems.at[w]))
        copies[-1].start()
    for copy in copies:
        copy.wait()


def tally_kernel(groups, places, *refs):
    xs, refs = chunks(groups, refs)
    coded, kept, kept_out = refs
    half = kept.shape[1] // 2
    for i in range(2):
        rows = block(i, half)
        kept_out[:, rows] = kept[:, rows] + code_sum(places, xs, coded, rows)


def code_kernel(groups, places, core, *refs):
    xs, refs = chunks(groups, refs)
    coded, kept, kept_out, mine, other = refs
    rows = kept.shape[1] // 2

    def half(index, out):
        columns = pl.ds(pl.multiple_of(index * rows, rows), rows)
        value = kept[:, columns] + code_sum(places, xs, coded, columns)
        kept_out[:, columns] = value
        for t in range(rows // 128):
            out[block(t, value.shape[0]), :] = value[:, block(t, 128)]

    half(1 - core[0], other)
    half(core[0], mine)


def fresh_kernel(groups, band, places, *refs):
    count = sum(groups)
    xs, refs = refs[:count], refs[count:]
    grad_out, total, kept, stacked, fresh, x_in, g_in, total_in, kept_in, staged, sems, out_sems = refs
    rows, columns = total.shape
    steps, wides = rows // TILE, columns // TILE
    tokens = x_in.shape[0] // len(groups)
    ends = []
    ready = [[0] * wides for _ in range(steps)]
    for i in range(steps):
        span, start = block(i, TILE), 0
        for x in xs:
            ends.append((x.at[:, span], x_in.at[start : start + x.shape[0], span]))
            start += x.shape[0]
        for w in range(wides):
            wide = block(w, TILE)
            for s in range(len(groups) if i == 0 else 0):
                ends.append((grad_out.at[tokens_of(places[s], tokens), wide], g_in.at[block(s, tokens), wide]))
            ends.append((total.at[span, wide], total_in.at[span, wide]))
            if w == 0:
                ends.append((kept.at[:, span], kept_in.at[:, span]))
            ready[i][w] = len(ends)
    copies = [pltpu.make_async_copy(*pair, sems.at[i]) for i, pair in enumerate(ends)]
    for copy in copies:
        copy.start()
    waited, outs = 0, []
    for i in range(steps):
        span = block(i, TILE)
        for w in range(wides):
            for copy in copies[waited : ready[i][w]]:
                copy.wait()
            waited = ready[i][w]
            for b in range(w * TILE // GROUP, (w + 1) * TILE // GROUP):
                cols = block(b, GROUP)
                value = total_in[span, cols] + dot(x_in[:, span], g_in[:, cols], (0, 0))
                value = value - decode(kept_in[block(b, band), span], stacked[...])
                staged[span, cols] = value.astype(BF16)
        outs.append(pltpu.make_async_copy(staged.at[span], fresh.at[0, span], out_sems.at[i]))
        outs[-1].start()
    for out in outs:
        out.wait()


def save_kernel(kept, kept_out, sem):
    copy = pltpu.make_async_copy(kept, kept_out, sem)
    copy.start()
    copy.wait()


def join_kernel(mine, other, out, staged, sems):
    halves = [block(h, mine.shape[0] // 2) for h in range(2)]
    copies = []
    for h, half in enumerate(halves):
        staged[half, :] = mine[half, :] + other[half, :]
        copies.append(pltpu.make_async_copy(staged.at[half], out.at[half], sems.at[h]))
        copies[-1].start()
    for copy in copies:
        copy.wait()


def part_kernel(chips, parts, spread):
    rows = parts.shape[0] // chips
    value = parts[:rows, :]
    for i in range(1, chips):
        value = value + parts[block(i, rows), :]
    largest = jnp.maximum(jnp.max(jnp.abs(value), axis=0, keepdims=True), 2.0**-100)
    power = jnp.ceil(jnp.log2(largest))
    level = jnp.round(value * jnp.exp2(15.0 - power))
    level = jnp.clip(level, -32767.0, 32767.0).astype(jnp.int32).astype(jnp.int16)
    power = jnp.broadcast_to(power, (PAD, value.shape[1])).astype(jnp.int32).astype(jnp.int16)
    for i in range(chips):
        start = i * (rows + PAD)
        spread[start : start + rows, :] = level
        spread[start + rows : start + rows + PAD, :] = power


def update_kernel(band, chips, where, whole, stacked, *refs):
    update, staged, sems = refs[-3:]
    rows = whole.shape[0] // chips - PAD
    values = []
    for i in range(chips):
        start = i * (rows + PAD)
        level = whole[start : start + rows, :].astype(jnp.int32).astype(F32)
        power = whole[start + rows : start + rows + PAD, :].astype(jnp.int32).astype(F32)[:1]
        values.append(level * jnp.exp2(power - 15.0))
    value = jnp.concatenate(values, axis=0)
    tiles = staged.shape[0] // 128
    kept = value.shape[0] // tiles
    span = pl.ds(pl.multiple_of(where[0] * staged.shape[0], staged.shape[0]), staged.shape[0])
    outs = []
    for b in range(staged.shape[1] // GROUP):
        parts = [value[t * kept + b * band : t * kept + (b + 1) * band] for t in range(tiles)]
        wide = block(b, GROUP)
        staged[:, wide] = decode(jnp.concatenate(parts, axis=1), stacked[...]).astype(BF16)
        outs.append(pltpu.make_async_copy(staged.at[:, wide], update.at[span, wide], sems.at[b]))
        outs[-1].start()
    for out in outs:
        out.wait()


VMEM = pl.BlockSpec(memory_space=pltpu.VMEM)
SMEM = pl.BlockSpec(memory_space=pltpu.SMEM)
ANY = pl.BlockSpec(memory_space=pl.ANY)
HBM = pl.BlockSpec(memory_space=pltpu.HBM)


def params(mib):
    return pltpu.CompilerParams(vmem_limit_bytes=mib << 20)


def held(value):
    return pltpu.with_memory_space_constraint(value, pltpu.VMEM)


def far(value):
    return pltpu.with_memory_space_constraint(value, pltpu.HBM)


def estimate(flops, size):
    return pl.CostEstimate(flops=flops, bytes_accessed=size, transcendentals=0)


def load(place, grad_out, momentum, pair, x_rows, band):
    tokens, columns = grad_out.shape
    rows = momentum.shape[1]
    kept = columns // GROUP * band
    return pl.pallas_call(
        functools.partial(load_kernel, band),
        in_specs=[SMEM, ANY, ANY, VMEM, ANY],
        out_specs=[VMEM] * 5,
        out_shape=[
            pltpu.VMEM((2 * kept, tokens), BF16),
            pltpu.VMEM((kept, rows), F32),
            pltpu.VMEM(x_rows.shape, BF16),
            pltpu.VMEM(grad_out.shape, BF16),
            pltpu.VMEM((rows, columns), F32),
        ],
        scratch_shapes=[pltpu.VMEM((rows, columns), BF16), pltpu.SemaphoreType.DMA((4,))],
        compiler_params=params(16),
        cost_estimate=estimate(2 * columns * (tokens + rows) * 256, 2 * columns * (tokens + rows)),
        name="load",
    )(place, far(grad_out), far(momentum), pair, far(x_rows))


def flat(chunks):
    pieces = [piece for chunk in chunks for piece in chunk]
    return tuple(map(len, chunks)), pieces, len(pieces), sum(piece.shape[0] for piece in pieces)


def add(span, places, xs, grad_in, base, total=None):
    groups, xs, count, tokens = flat(xs)
    shape = base.shape
    rows = span.stop - span.start
    others = [] if total is None else [far(total)]
    return pl.pallas_call(
        functools.partial(add_kernel, groups, span),
        in_specs=[SMEM] + [VMEM] * (count + 2) + [ANY] * len(others),
        out_specs=ANY,
        out_shape=pltpu.HBM(shape, F32),
        input_output_aliases={count + 3: 0} if others else {},
        scratch_shapes=[pltpu.VMEM((rows, shape[1]), F32), pltpu.SemaphoreType.DMA((shape[1] // TILE,))],
        compiler_params=params(16),
        cost_estimate=estimate(2 * tokens * rows * shape[1], rows * shape[1] * 4),
        name="add",
    )(places, *[held(x) for x in xs], held(grad_in), held(base), *others)


def tally(places, xs, coded, kept):
    groups, xs, count, tokens = flat(xs)
    size, rows = kept.shape
    return pl.pallas_call(
        functools.partial(tally_kernel, groups),
        in_specs=[SMEM] + [VMEM] * (count + 2),
        out_specs=VMEM,
        out_shape=pltpu.VMEM(kept.shape, F32),
        compiler_params=params(16),
        cost_estimate=estimate(2 * tokens * rows * size * 2, 0),
        name="tally",
    )(places, *[held(x) for x in xs], held(coded), held(kept))


def code(places, core, xs, coded, kept):
    groups, xs, count, tokens = flat(xs)
    size, rows = kept.shape
    out = jax.ShapeDtypeStruct((size * rows // 256, 128), F32)
    return pl.pallas_call(
        functools.partial(code_kernel, groups),
        in_specs=[SMEM, SMEM] + [VMEM] * (count + 2),
        out_specs=[VMEM] * 3,
        out_shape=[pltpu.VMEM(kept.shape, F32), pltpu.VMEM(out.shape, F32), pltpu.VMEM(out.shape, F32)],
        compiler_params=params(16),
        cost_estimate=estimate(2 * tokens * rows * size * 2, 0),
        name="code",
    )(places, core, *[held(x) for x in xs], held(coded), held(kept))


def finish(places, xs, grad_out, total, kept, stacked, band):
    groups, xs, count, tokens = flat(xs)
    rows, columns = total.shape
    steps, wides = rows // TILE, columns // TILE
    loads = (count + 1) * steps + wides * (len(groups) + steps)
    return pl.pallas_call(
        functools.partial(fresh_kernel, groups, band),
        in_specs=[SMEM] + [ANY] * (count + 3) + [VMEM],
        out_specs=ANY,
        out_shape=jax.ShapeDtypeStruct((1, rows, columns), BF16),
        scratch_shapes=[
            pltpu.VMEM((tokens, rows), BF16),
            pltpu.VMEM((tokens, columns), BF16),
            pltpu.VMEM(total.shape, F32),
            pltpu.VMEM(kept.shape, F32),
            pltpu.VMEM((rows, columns), BF16),
            pltpu.SemaphoreType.DMA((loads,)),
            pltpu.SemaphoreType.DMA((steps,)),
        ],
        compiler_params=params(24),
        cost_estimate=estimate(4 * tokens * rows * columns, rows * columns * 6),
        name="finish",
    )(places, *map(far, xs), far(grad_out), far(total), far(kept), stacked)


def save(kept):
    return pl.pallas_call(
        save_kernel,
        in_specs=[VMEM],
        out_specs=ANY,
        out_shape=pltpu.HBM(kept.shape, F32),
        scratch_shapes=[pltpu.SemaphoreType.DMA],
        compiler_params=params(4),
        cost_estimate=estimate(0, kept.size * 4),
        name="save",
    )(held(kept))


def join(mine, other):
    return pl.pallas_call(
        join_kernel,
        in_specs=[VMEM] * 2,
        out_specs=ANY,
        out_shape=pltpu.HBM(mine.shape, F32),
        scratch_shapes=[pltpu.VMEM(mine.shape, F32), pltpu.SemaphoreType.DMA((2,))],
        compiler_params=params(4),
        name="join",
    )(held(mine), held(other))


def sum_parts(parts, chips):
    return pl.pallas_call(
        functools.partial(part_kernel, chips),
        in_specs=[VMEM],
        out_specs=VMEM,
        out_shape=pltpu.VMEM((parts.shape[0] + chips * PAD, parts.shape[1]), jnp.int16),
        compiler_params=params(16),
        name="sum_parts",
    )(held(parts))


def make_update(where, whole, stacked, band, rows, columns, update=None):
    others = [] if update is None else [update]
    return pl.pallas_call(
        functools.partial(update_kernel, band, 16),
        in_specs=[SMEM, VMEM, VMEM] + [ANY] * len(others),
        out_specs=ANY,
        out_shape=jax.ShapeDtypeStruct((rows, columns), BF16),
        input_output_aliases={3: 0} if others else {},
        scratch_shapes=[pltpu.VMEM((rows // 2, columns), BF16), pltpu.SemaphoreType.DMA((columns // GROUP,))],
        compiler_params=params(16),
        cost_estimate=estimate(rows * columns * 96, rows * columns),
        name="update",
    )(where, held(whole), held(stacked), *others)


def shards(x_rows, grad_out, momentum, band_index):
    band = band_index.shape[0]
    basis = dct_rows(band_index, GROUP)
    rounded = lax.reduce_precision(basis, 8, 7)
    high, low = rounded.astype(BF16), (basis - rounded).astype(BF16)
    pair = jnp.concatenate([high, low], axis=0)
    stacked = jnp.concatenate([high, high, low], axis=0)

    y, xl = lax.axis_index("y"), lax.axis_index("xl")
    core = lax.axis_index("core").astype(jnp.int32).reshape(1)

    def places(*steps):
        return jnp.stack([((y + dy) % 4) * 2 + (xl + dx) % 2 for dy, dx in steps]).astype(jnp.int32)

    def across(v):
        return lax.ppermute(v, "xl", PAIR)

    def from_above(v):
        return lax.ppermute(v, "y", ring(4, -1))

    def from_below(v):
        return lax.ppermute(v, "y", ring(4, 1))

    first = places((0, 0))
    near = places((0, 1), (1, 0), (3, 0))
    middle = places((1, 1), (3, 1), (2, 0))
    last = places((2, 1))
    ends = places((1, 1), (3, 1), (2, 0), (2, 1))
    apart = 1 - core
    pair, stacked, first, near, middle, last, ends, core, apart = lax.optimization_barrier(
        (pair, stacked, first, near, middle, last, ends, core, apart)
    )
    with jax.named_scope("gather_near"):
        yp, xn, ym = from_above(x_rows), across(x_rows), from_below(x_rows)
        loaded = load(first, grad_out, momentum, pair, x_rows, band)
        yp, (coded, kept, own, grad_in, base) = lax.optimization_barrier((yp, loaded))
        xn, ym = lax.optimization_barrier((xn, ym))
    half = yp.shape[0] // 2
    with jax.named_scope("gather_middle"):
        y2 = [from_above(yp[:half])]
        xyp = across(yp)
        y2.append(from_above(yp[half:]))
        xym = [from_below(xn[half:])]
        xym.insert(0, from_below(xn[:half]))
    rows = momentum.shape[1]
    close = [[xn], [yp], [ym]]
    total = add(slice(0, rows // 2), near, close, grad_in, base)
    y2[0], total = lax.optimization_barrier((y2[0], total))
    with jax.named_scope("gather_far"):
        xy2 = [across(y2[0]), from_below(xym[1])]
    total = add(slice(rows // 2, rows), near, close, grad_in, base, total)
    kept = tally(near, close, coded, kept)
    kept = tally(middle, [[xyp], xym, y2], coded, kept)
    kept, total = lax.optimization_barrier((kept, total))
    kept, mine, other = code(last, core, [xy2], coded, kept)
    with jax.named_scope("sum_core"):
        other, kept = lax.optimization_barrier((lax.ppermute(other, "core", PAIR), save(kept)))
        mine = join(mine, other)
    with jax.named_scope("sum_chips"):
        parts = lax.all_to_all(mine, ("z", "xh"), 0, 0, tiled=True)
    fresh = finish(ends, [[xyp], xym, y2, xy2], grad_out, total, kept, stacked, band)
    parts, fresh = lax.optimization_barrier((parts, fresh))
    with jax.named_scope("spread_chips"):
        whole = lax.all_to_all(sum_parts(parts, 16), ("z", "xh"), 0, 0, tiled=True)
    with jax.named_scope("spread_core"):
        other = lax.ppermute(whole, "core", PAIR)
    update = make_update(core, whole, stacked, band, rows, grad_out.shape[1])
    return fresh, make_update(apart, other, stacked, band, rows, grad_out.shape[1], update)


def solution(mesh):
    fine = Mesh(mesh.devices.reshape(8, 2, 2, 4, 2), ("z", "xh", "core", "y", "xl"))
    rep, col = ("z", "xh", "core"), ("y", "xl")
    return jax.shard_map(
        shards,
        mesh=fine,
        in_specs=(P(rep + col, None), P(rep, col), P(rep, None, col), P()),
        out_specs=(P(rep, None, col), P(None, col)),
        check_vma=False,
    )
```
